32 devices in a mesh: region: 4 (over x, core), unit: 8 (over z, y).
Axes of the slice: x: 2, y: 2, z: 4, core: 2. Of those that a mesh axis runs over, the one named last changes fastest.
Arguments:
- noisy: bfloat16 [8192, 2048], P(('region', 'unit')), may hold values from -6 to 6
- strategy: bfloat16 [2048, 2048], replicated, may hold values from -0.125 to 0.125
- county_hist: float32 [256, 2048], P(('region', 'unit')), may hold values from -24 to 24
- tract_county: int32 [8192], P(('region', 'unit')), may hold values from 0 to 255, as said below
- tract_owner: int32 [8192, 1], P(('region', 'unit')), may hold values from 0 to 31; in each aligned block of 256 rows (0 to 255, 256 to 511, ...) at most 16 rows name the same one
Outputs:
- released: bfloat16 [8192, 2048], P(('region', 'unit'))
- relaid: float32 [16384, 2048], P(('region', 'unit'))
The draws below stay inside these ranges and needn't reach their ends.
Inputs may be any that keep to these rules, and one draw needn't show every extreme that they name: `tract_county`: every county has at least one tract; the tracts of region r (rows r * 256 * 8 onward) lie in counties of region r (rows r * 8 * 8 onward of county_hist). `tract_owner`: among the 256 rows of one device no owner appears more than 16 times, and some owner appears exactly 16 times.
All inputs are finite; a program needn't handle non-finite values.
Results may differ from the reference program's by a relative error of at most 0.005.
Values sent between devices are 32-bit elements; how exact they have to be, the bound alone decides.
A program may use at most 64 MiB of HBM per device.

```python
import math
import jax
import jax.numpy as jnp
import numpy as np
from jax import lax

H = 2048
K = 2048
TR_DEV = 256
CTY_DEV = 8
ITERS = 2
TRACTS = 8192
COUNTIES = 256
CAP = 16
N_REGION = 4
N_UNIT = 8
DEVICES = 32


def draw_tract_county(key, part):
    tract_region = TR_DEV * N_UNIT
    county_region = CTY_DEV * N_UNIT

    def region_draw(region_key):
        first_key, second_key, third_key = jax.random.split(region_key, 3)
        order_rank = jax.random.permutation(first_key, tract_region)
        left_pick = jax.random.randint(second_key, (tract_region,), 0, county_region)
        right_pick = jax.random.randint(third_key, (tract_region,), 0, county_region)
        skewed = jnp.minimum(left_pick, right_pick)
        return jnp.where(order_rank < county_region, order_rank, skewed).astype(jnp.int32)
    region_keys = jax.random.split(jax.random.fold_in(key, 17), N_REGION)
    local_ids = jax.vmap(region_draw)(region_keys)
    offsets = (jnp.arange(N_REGION, dtype=jnp.int32) * county_region)[:, None]
    return (local_ids + offsets).reshape(-1).astype(jnp.int32)


def levels(rng, shape, pieces, least, largest):
    loudness = 1.0
    for position, blocks in pieces:
        steps = jax.random.uniform(jax.random.fold_in(jax.random.fold_in(rng, 6), position), (blocks,), jnp.float32, least / len(pieces), largest / len(pieces))
        loudness = loudness * jnp.repeat(jnp.exp(steps), shape[position] // blocks).reshape((-1,) + (1,) * (len(shape) - 1 - position))
    return loudness


def deal_out(own_key, own, number, rows, amount, top, reach, skew):
    order = jax.random.permutation(own_key, amount)
    crowded, common = shares(amount, rows * top, reach, skew, True), shares(amount, rows * top, reach, skew, False)
    places = jnp.arange(amount)

    def named(sizes, turn):
        used = int((sizes > 0).sum())
        fixed = max(1, used // 4)
        shifted = fixed + (places - fixed + turn * (used - fixed)) % max(1, amount - fixed)
        return jnp.zeros((amount,), jnp.int32).at[order[jnp.where(places < fixed, places, shifted)]].set(jnp.asarray(sizes, jnp.int32))

    sizes = jnp.where(number % 4 == 0, named(crowded, number // 4), named(common, number - number // 4 - 1))
    mixed = jax.random.permutation(jax.random.fold_in(own, 3), amount)
    donor, receiver = mixed[0:amount // 2 * 2:2], mixed[1:amount // 2 * 2:2]
    room = jnp.minimum(sizes[donor] - 1, reach - sizes[receiver]) // 2
    room = jnp.where((donor == order[0]) | (receiver == order[0]) | (sizes[receiver] == 0), 0, jnp.maximum(room, 0))
    shifted = jax.random.randint(jax.random.fold_in(own, 4), (amount // 2,), 0, 1 << 20) % (room + 1)
    sizes = sizes.at[donor].add(-shifted).at[receiver].add(shifted)
    members = jnp.searchsorted(jnp.cumsum(sizes), jnp.arange(rows * top), side="right").astype(jnp.int32)
    table = members.reshape(top, rows).T
    table = table[jax.random.permutation(jax.random.fold_in(own, 1), rows)]
    turn = jax.random.randint(jax.random.fold_in(own, 2), (rows, 1), 0, top)
    return jnp.take_along_axis(table, (jnp.arange(top)[None, :] + turn) % top, axis=1)


def shares(count, total, most, lean, full):
    weights = [(1 << 20) // math.isqrt(grade ** lean) + 1 for grade in range(1, count + 1)]
    largest = most if full else min(most, max(-(-total // count), total * weights[0] // sum(weights)))
    least = 1 if total - largest >= count - 1 else 0
    counts, rest = [largest] + [least] * (count - 1), total - largest - least * (count - 1)
    while rest > 0:
        free = [i for i in range(1, count) if counts[i] < largest] or [i for i in range(1, count) if counts[i] < most]
        pool, remaining = sum([weights[i] for i in free]), rest
        for i in free:
            addition = min(most - counts[i], max(1, remaining * weights[i] // pool), rest)
            counts[i] = counts[i] + addition
            rest = rest - addition
    return np.array(counts)


def normal_values(key, shape, deviation, limit, cuts=(), held_as=jnp.bfloat16):
    values = jax.random.normal(key, shape, jnp.float32) * deviation
    if len(cuts) > 0:
        values = levels(key, shape, cuts, -0.22, 0.18) * values
    return jnp.clip(values, min=-limit, max=limit).astype(held_as)


def setup_inputs(seed: int = 0) -> dict:
    key_of = jax.random.split(jax.random.key(seed), 6)
    noisy = normal_values(key_of[0], (TRACTS, K), 1.0, 6.0, ((0, 32),))
    strategy = normal_values(key_of[1], (H, K), H ** -0.5, 0.125)
    county_hist = normal_values(key_of[2], (COUNTIES, H), 4.0, 24.0, ((0, 32),), jnp.float32)
    tract_county = draw_tract_county(jax.random.fold_in(key_of[5], 71), 0)
    tract_owner_keys = jax.random.split(jax.random.fold_in(key_of[4], 1), TRACTS // TR_DEV)
    tract_owner_turns = jax.random.permutation(jax.random.fold_in(key_of[4], 3), TRACTS // TR_DEV)
    tract_owner = jax.vmap(lambda own, number: deal_out(jax.random.fold_in(key_of[4], 2), own, number, TR_DEV, DEVICES, 1, CAP, 2))(tract_owner_keys, tract_owner_turns).reshape((TRACTS, 1))
    return dict(noisy=noisy, strategy=strategy, county_hist=county_hist, tract_county=tract_county, tract_owner=tract_owner)


step_size = 0.25


def reference(noisy, strategy, county_hist, tract_county, tract_owner):
    tracts = noisy.shape[0]
    tract_count = jax.ops.segment_sum(jnp.ones((tracts,), jnp.float32), tract_county, num_segments=COUNTIES)
    estimate = jnp.zeros((tracts, H), jnp.float32)
    for iteration in range(ITERS):
        answers = jnp.dot(estimate.astype(jnp.bfloat16), strategy, preferred_element_type=jnp.float32)
        misfit = (answers - noisy.astype(jnp.float32)).astype(jnp.bfloat16)
        gradient = lax.dot_general(misfit, strategy, (((1,), (1,)), ((), ())), preferred_element_type=jnp.float32)
        stepped = estimate - step_size * gradient
        child_total = jax.ops.segment_sum(stepped, tract_county, num_segments=COUNTIES)
        parent_gap = (county_hist - child_total) / tract_count[:, None]
        estimate = stepped + parent_gap[tract_county]
    released = jnp.dot(estimate.astype(jnp.bfloat16), strategy, preferred_element_type=jnp.float32).astype(jnp.bfloat16)
    owners = tract_owner[:, 0].reshape(DEVICES, TR_DEV)
    owner_hits = (owners[:, :, None] == jnp.arange(DEVICES, dtype=jnp.int32)[None, None, :]).astype(jnp.int32)
    slot_index = jnp.sum((jnp.cumsum(owner_hits, axis=1) - owner_hits) * owner_hits, axis=2)
    source = jnp.arange(DEVICES, dtype=jnp.int32)[:, None]
    target = (owners * (DEVICES * CAP) + source * CAP + slot_index).astype(jnp.int32)
    relaid = jnp.zeros((DEVICES * DEVICES * CAP, H), jnp.float32).at[target.reshape(-1)].set(estimate)
    return released, relaid
```

```python
import functools

import jax
import jax.numpy as jnp
from jax import lax
from jax.experimental import pallas as pl
from jax.experimental.pallas import tpu as pltpu
from jax.sharding import PartitionSpec as P

STEP = 0.25
TILE = 256
LANES = 128
MESH = pl.DeviceIdType.MESH
f32, bf16, i32 = jnp.float32, jnp.bfloat16, jnp.int32


def dot_nn(a, b):
    return lax.dot_general(a, b, (((1,), (0,)), ((), ())), preferred_element_type=f32)


def dot_nt(a, b):
    return lax.dot_general(a, b, (((1,), (1,)), ((), ())), preferred_element_type=f32)


def halves(x):
    high = x.astype(bf16)
    return high, (x - high.astype(f32)).astype(bf16)


def kernel(
    regions,
    units,
    noisy,
    strategy,
    hist,
    county_row,
    county_col,
    owner_row,
    released,
    relaid,
    matrix,
    field,
    rounded,
    misfit,
    partial,
    gathered,
    gaps,
    slots,
    load_sem,
    sum_send,
    sum_recv,
    gap_send,
    gap_recv,
    row_send,
    row_recv,
    own_sem,
):
    devices = regions * units
    region, unit = lax.axis_index("region"), lax.axis_index("unit")
    me = region * units + unit
    rows, queries = noisy.shape
    width = strategy.shape[0]
    block = hist.shape[0]
    counties = units * block
    pitch = slots.shape[1]

    def load(i):
        part = pl.ds(pl.multiple_of(i * TILE, TILE), TILE)
        return pltpu.make_async_copy(strategy.at[part], matrix.at[part], load_sem.at[i])

    lax.fori_loop(0, width // TILE, lambda i, c: (load(i).start(), c)[1], 0)

    barrier = pltpu.get_barrier_semaphore()

    def greet(k, c):
        peer = lax.rem(me + k, devices)
        pl.semaphore_signal(
            barrier, inc=1, device_id=(peer // units, lax.rem(peer, units)), device_id_type=MESH
        )
        return c

    lax.fori_loop(1, devices, greet, 0)

    def columns(i):
        return pl.ds(pl.multiple_of(i * TILE, TILE), TILE)

    def first(i, c):
        load(i).wait()
        value = STEP * dot_nt(noisy[...], matrix[columns(i), :])
        field[:, columns(i)] = value
        rounded[:, columns(i)] = value.astype(bf16)
        return c

    lax.fori_loop(0, width // TILE, first, 0)

    def second(i, c):
        misfit[:, columns(i)] = dot_nn(rounded[...], matrix[:, columns(i)]).astype(bf16)
        return c

    lax.fori_loop(0, queries // TILE, second, 0)

    local_row = county_row[...] - region * counties
    member_row = (
        lax.broadcasted_iota(i32, (counties, rows), 0) == jnp.broadcast_to(local_row, (counties, rows))
    )
    member_sum = member_row.astype(f32).astype(bf16)

    def third(i, c):
        value = 2.0 * field[:, columns(i)] - STEP * dot_nt(misfit[...], matrix[columns(i), :])
        field[:, columns(i)] = value
        high, low = halves(value)
        total = dot_nn(member_sum, high) + dot_nn(member_sum, low)
        partial[:, :, columns(i)] = total.reshape(units, block, TILE)
        return c

    lax.fori_loop(0, width // TILE, third, 0)
    tally = jnp.sum(member_row.astype(f32), axis=1, keepdims=True)
    partial[:, :, width:] = jnp.broadcast_to(tally, (counties, LANES)).reshape(units, block, LANES)

    pl.semaphore_wait(barrier, devices - 1)

    def to_unit(k):
        return lax.rem(unit + k, units), lax.rem(unit + units - k, units)

    def sum_copy(k):
        peer, _ = to_unit(k)
        return pltpu.make_async_remote_copy(
            src_ref=partial.at[peer],
            dst_ref=gathered.at[k],
            send_sem=sum_send.at[k],
            recv_sem=sum_recv.at[k],
            device_id=(region, peer),
            device_id_type=MESH,
        )

    for k in range(1, units):
        sum_copy(k).start()

    owners = owner_row[...]
    hits = lax.broadcasted_iota(i32, (devices, rows), 0) == jnp.broadcast_to(owners, (devices, rows))
    before = lax.broadcasted_iota(i32, (rows, rows), 0) < lax.broadcasted_iota(i32, (rows, rows), 1)
    earlier = dot_nn(hits.astype(f32).astype(bf16), before.astype(f32).astype(bf16))
    slot = jnp.sum(earlier * hits.astype(f32), axis=0, keepdims=True).astype(i32)
    target = owners * pitch + slot
    place = (
        lax.broadcasted_iota(i32, (devices * pitch, rows), 0)
        == jnp.broadcast_to(target, (devices * pitch, rows))
    ).astype(f32).astype(bf16)
    local_col = county_col[...] - region * counties
    member_col = (
        lax.broadcasted_iota(i32, (rows, counties), 1) == jnp.broadcast_to(local_col, (rows, counties))
    ).astype(f32).astype(bf16)

    for k in range(1, units):
        sum_copy(k).wait()
    total = partial[unit]
    for k in range(1, units):
        total = total + gathered[k]
    gaps[unit] = (hist[...] - total[:, :width]) / total[:, width : width + 1]

    def gap_copy(k, slot_at):
        peer, _ = to_unit(k)
        return pltpu.make_async_remote_copy(
            src_ref=gaps.at[slot_at],
            dst_ref=gaps.at[slot_at],
            send_sem=gap_send.at[k],
            recv_sem=gap_recv.at[k],
            device_id=(region, peer),
            device_id_type=MESH,
        )

    for k in range(1, units):
        gap_copy(k, unit).start()
    for k in range(1, units):
        gap_copy(k, unit).wait_send()
        gap_copy(k, to_unit(k)[1]).wait_recv()

    def last(i, c):
        high, low = halves(gaps[:, :, columns(i)].reshape(counties, TILE))
        value = field[:, columns(i)] + (dot_nn(member_col, high) + dot_nn(member_col, low))
        high, low = halves(value)
        rounded[:, columns(i)] = high
        placed = dot_nn(place, high) + dot_nn(place, low)
        slots[:, :, columns(i)] = placed.reshape(devices, pitch, TILE)
        return c

    lax.fori_loop(0, width // TILE, last, 0)

    def row_copy(k):
        peer = lax.rem(me + k, devices)
        return pltpu.make_async_remote_copy(
            src_ref=slots.at[peer],
            dst_ref=relaid.at[me],
            send_sem=row_send.at[k],
            recv_sem=row_recv.at[k],
            device_id=(peer // units, lax.rem(peer, units)),
            device_id_type=MESH,
        )

    lax.fori_loop(1, devices, lambda k, c: (row_copy(k).start(), c)[1], 0)
    own = pltpu.make_async_copy(slots.at[me], relaid.at[me], own_sem)
    own.start()

    def release(i, c):
        released[:, columns(i)] = dot_nn(rounded[...], matrix[:, columns(i)]).astype(bf16)
        return c

    lax.fori_loop(0, queries // TILE, release, 0)
    own.wait()

    def finish(k, c):
        row_copy(k).wait_send()
        source = lax.rem(me + devices - k, devices)
        pltpu.make_async_remote_copy(
            src_ref=slots.at[me],
            dst_ref=relaid.at[source],
            send_sem=row_send.at[k],
            recv_sem=row_recv.at[k],
            device_id=(source // units, lax.rem(source, units)),
            device_id_type=MESH,
        ).wait_recv()
        return c

    lax.fori_loop(1, devices, finish, 0)


def local(noisy, strategy, county_hist, tract_county, tract_owner):
    units, regions = lax.axis_size("unit"), lax.axis_size("region")
    devices = units * regions
    rows, queries = noisy.shape
    width = strategy.shape[0]
    block = county_hist.shape[0]
    capacity = 2 * rows // devices
    pitch = -(-capacity // 8) * 8
    vmem = pl.BlockSpec(memory_space=pltpu.VMEM)
    released, relaid = pl.pallas_call(
        functools.partial(kernel, regions, units),
        out_shape=(
            jax.ShapeDtypeStruct((rows, queries), bf16),
            jax.ShapeDtypeStruct((devices, pitch, width), f32),
        ),
        in_specs=[vmem, pl.BlockSpec(memory_space=pl.ANY), vmem, vmem, vmem, vmem],
        out_specs=(vmem, pl.BlockSpec(memory_space=pl.ANY)),
        scratch_shapes=[
            pltpu.VMEM((width, queries), bf16),
            pltpu.VMEM((rows, width), f32),
            pltpu.VMEM((rows, width), bf16),
            pltpu.VMEM((rows, queries), bf16),
            pltpu.VMEM((units, block, width + LANES), f32),
            pltpu.VMEM((units, block, width + LANES), f32),
            pltpu.VMEM((units, block, width), f32),
            pltpu.VMEM((devices, pitch, width), f32),
            pltpu.SemaphoreType.DMA((width // TILE,)),
            pltpu.SemaphoreType.DMA((units,)),
            pltpu.SemaphoreType.DMA((units,)),
            pltpu.SemaphoreType.DMA((units,)),
            pltpu.SemaphoreType.DMA((units,)),
            pltpu.SemaphoreType.DMA((devices,)),
            pltpu.SemaphoreType.DMA((devices,)),
            pltpu.SemaphoreType.DMA,
        ],
        compiler_params=pltpu.CompilerParams(
            collective_id=0, has_side_effects=True, vmem_limit_bytes=50 * 2**20
        ),
    )(
        noisy,
        strategy,
        county_hist,
        tract_county.reshape(1, rows),
        tract_county.reshape(rows, 1),
        tract_owner.reshape(1, rows),
    )
    return released, relaid[:, :capacity].reshape(devices * capacity, width)


def solution(mesh):
    both = ("region", "unit")
    in_specs = (P(both, None), P(), P(both, None), P(both), P(both, None))
    return jax.shard_map(
        local, mesh=mesh, in_specs=in_specs, out_specs=(P(both, None), P(both, None)), check_vma=False
    )
```

```python
import functools

import jax
import jax.numpy as jnp
from jax import lax
from jax.experimental import pallas as pl
from jax.experimental.pallas import tpu as pltpu
from jax.sharding import PartitionSpec as P

STEP = 0.25
TILE = 256
LANES = 128
MESH = pl.DeviceIdType.MESH
f32, bf16, i32 = jnp.float32, jnp.bfloat16, jnp.int32


def dot_nn(a, b):
    return lax.dot_general(a, b, (((1,), (0,)), ((), ())), preferred_element_type=f32)


def dot_nt(a, b):
    return lax.dot_general(a, b, (((1,), (1,)), ((), ())), preferred_element_type=f32)


def halves(x):
    high = x.astype(bf16)
    return high, (x - high.astype(f32)).astype(bf16)


def kernel(
    regions,
    units,
    noisy_in,
    strategy,
    hist_in,
    county_in,
    owner_in,
    released,
    relaid,
    noisy,
    hist,
    county_row,
    owner_row,
    matrix,
    turned,
    field,
    rounded,
    misfit,
    partial,
    gathered,
    gaps,
    slots,
    mean_step,
    mean_misfit,
    input_sem,
    load_sem,
    sum_send,
    sum_recv,
    gap_send,
    gap_recv,
    row_send,
    row_recv,
    own_sem,
):
    devices = regions * units
    region, unit = lax.axis_index("region"), lax.axis_index("unit")
    me = region * units + unit
    rows, queries = noisy.shape
    width = strategy.shape[0]
    block = hist.shape[0]
    counties = units * block
    pitch = slots.shape[1]

    inputs = [
        pltpu.make_async_copy(source, target, input_sem.at[i])
        for i, (source, target) in enumerate(
            [(county_in, county_row), (noisy_in, noisy), (hist_in, hist), (owner_in, owner_row)]
        )
    ]
    for copy in inputs:
        copy.start()

    def load(i):
        part = pl.ds(pl.multiple_of(i * TILE, TILE), TILE)
        return pltpu.make_async_copy(strategy.at[part], matrix.at[part], load_sem.at[i])

    lax.fori_loop(0, width // TILE, lambda i, c: (load(i).start(), c)[1], 0)

    barrier = pltpu.get_barrier_semaphore()

    def greet(k, c):
        peer = lax.rem(me + k, devices)
        pl.semaphore_signal(
            barrier, inc=1, device_id=(peer // units, lax.rem(peer, units)), device_id_type=MESH
        )
        return c

    lax.fori_loop(1, devices, greet, 0)

    def columns(i):
        return pl.ds(pl.multiple_of(i * TILE, TILE), TILE)

    for copy in inputs:
        copy.wait()
    local_row = county_row[...] - region * counties
    member_row = (
        lax.broadcasted_iota(i32, (counties, rows), 0) == jnp.broadcast_to(local_row, (counties, rows))
    )
    member_sum = member_row.astype(f32).astype(bf16)


    def sums(i, c):
        partial[:, :, columns(i)] = dot_nn(member_sum, noisy[:, columns(i)]).reshape(
            units, block, TILE
        )
        return c

    lax.fori_loop(0, queries // TILE, sums, 0)
    tally = jnp.sum(member_row.astype(f32), axis=1, keepdims=True)
    partial[:, :, queries:] = jnp.broadcast_to(tally, (counties, LANES)).reshape(units, block, LANES)

    pl.semaphore_wait(barrier, devices - 1)

    def to_unit(k):
        return lax.rem(unit + k, units), lax.rem(unit + units - k, units)

    def sum_copy(k):
        peer, _ = to_unit(k)
        return pltpu.make_async_remote_copy(
            src_ref=partial.at[peer],
            dst_ref=gathered.at[k],
            send_sem=sum_send.at[k],
            recv_sem=sum_recv.at[k],
            device_id=(region, peer),
            device_id_type=MESH,
        )

    for k in range(1, units):
        sum_copy(k).start()

    def first(i, c):
        load(i).wait()
        flipped = matrix[columns(i), :].T
        turned[:, columns(i)] = flipped
        value = STEP * dot_nn(noisy[...], flipped)
        field[:, columns(i)] = value
        rounded[:, columns(i)] = value.astype(bf16)
        return c

    lax.fori_loop(0, width // TILE, first, 0)

    def second(i, c):
        misfit[:, columns(i)] = dot_nn(rounded[...], matrix[:, columns(i)]).astype(bf16)
        return c

    lax.fori_loop(0, queries // TILE, second, 0)

    def third(i, c):
        field[:, columns(i)] = 2.0 * field[:, columns(i)] - STEP * dot_nn(
            misfit[...], turned[:, columns(i)]
        )
        return c

    lax.fori_loop(0, width // TILE, third, 0)
    owners = owner_row[...]
    hits = lax.broadcasted_iota(i32, (devices, rows), 0) == jnp.broadcast_to(owners, (devices, rows))
    before = lax.broadcasted_iota(i32, (rows, rows), 0) < lax.broadcasted_iota(i32, (rows, rows), 1)
    earlier = dot_nn(hits.astype(f32).astype(bf16), before.astype(f32).astype(bf16))
    slot = jnp.sum(earlier * hits.astype(f32), axis=0, keepdims=True).astype(i32)
    target = owners * pitch + slot
    place = (
        lax.broadcasted_iota(i32, (devices * pitch, rows), 0)
        == jnp.broadcast_to(target, (devices * pitch, rows))
    ).astype(f32).astype(bf16)
    diagonal = (
        lax.broadcasted_iota(i32, (rows, rows), 0) == lax.broadcasted_iota(i32, (rows, rows), 1)
    ).astype(f32).astype(bf16)
    member_col = dot_nt(diagonal, member_sum).astype(bf16)
    place_twice = jnp.concatenate([place, place], axis=1)
    county_place = dot_nt(place, member_sum).astype(bf16)
    county_twice = jnp.concatenate([county_place, county_place], axis=1)
    member_twice = jnp.concatenate([member_col, member_col], axis=1)

    for k in range(1, units):
        sum_copy(k).wait()
    total = partial[unit]
    for k in range(1, units):
        total = total + gathered[k]
    count = total[:, queries : queries + 1]
    mean = (total[:, :queries] / count).astype(bf16)

    def wide(i):
        return pl.ds(pl.multiple_of(i * 2 * TILE, 2 * TILE), 2 * TILE)

    def mean_first(i, c):
        mean_step[:, wide(i)] = STEP * dot_nn(mean, turned[:, wide(i)])
        return c

    lax.fori_loop(0, width // (2 * TILE), mean_first, 0)

    def mean_second(i, c):
        mean_misfit[:, wide(i)] = dot_nn(mean_step[...].astype(bf16), matrix[:, wide(i)])
        return c

    lax.fori_loop(0, queries // (2 * TILE), mean_second, 0)

    def mean_third(i, c):
        moved = 2.0 * mean_step[:, wide(i)] - STEP * dot_nn(
            mean_misfit[...].astype(bf16), turned[:, wide(i)]
        )
        gaps[unit, :, wide(i)] = hist[:, wide(i)] / count - moved
        return c

    lax.fori_loop(0, width // (2 * TILE), mean_third, 0)

    def gap_copy(k, slot_at):
        peer, _ = to_unit(k)
        return pltpu.make_async_remote_copy(
            src_ref=gaps.at[slot_at],
            dst_ref=gaps.at[slot_at],
            send_sem=gap_send.at[k],
            recv_sem=gap_recv.at[k],
            device_id=(region, peer),
            device_id_type=MESH,
        )

    for k in range(1, units):
        gap_copy(k, unit).start()
    def spread(i, c):
        pair = jnp.concatenate(halves(field[:, columns(i)]), axis=0)
        slots[:, :, columns(i)] = dot_nn(place_twice, pair).reshape(devices, pitch, TILE)
        return c

    lax.fori_loop(0, width // TILE, spread, 0)

    for k in range(1, units):
        gap_copy(k, unit).wait_send()
        gap_copy(k, to_unit(k)[1]).wait_recv()

    def last(i, c):
        pair = jnp.concatenate(halves(gaps[:, :, columns(i)].reshape(counties, TILE)), axis=0)
        slots[:, :, columns(i)] += dot_nn(county_twice, pair).reshape(devices, pitch, TILE)
        return c

    lax.fori_loop(0, width // TILE, last, 0)

    def row_copy(k):
        peer = lax.rem(me + k, devices)
        return pltpu.make_async_remote_copy(
            src_ref=slots.at[peer],
            dst_ref=relaid.at[me],
            send_sem=row_send.at[k],
            recv_sem=row_recv.at[k],
            device_id=(peer // units, lax.rem(peer, units)),
            device_id_type=MESH,
        )

    lax.fori_loop(1, devices, lambda k, c: (row_copy(k).start(), c)[1], 0)
    own = pltpu.make_async_copy(slots.at[me], relaid.at[me], own_sem)
    own.start()

    def settle(i, c):
        pair = jnp.concatenate(halves(gaps[:, :, columns(i)].reshape(counties, TILE)), axis=0)
        rounded[:, columns(i)] = (field[:, columns(i)] + dot_nn(member_twice, pair)).astype(bf16)
        return c

    lax.fori_loop(0, width // TILE, settle, 0)

    def release(i, c):
        released[:, columns(i)] = dot_nn(rounded[...], matrix[:, columns(i)]).astype(bf16)
        return c

    lax.fori_loop(0, queries // TILE, release, 0)
    own.wait()

    def finish(k, c):
        row_copy(k).wait_send()
        source = lax.rem(me + devices - k, devices)
        pltpu.make_async_remote_copy(
            src_ref=slots.at[me],
            dst_ref=relaid.at[source],
            send_sem=row_send.at[k],
            recv_sem=row_recv.at[k],
            device_id=(source // units, lax.rem(source, units)),
            device_id_type=MESH,
        ).wait_recv()
        return c

    lax.fori_loop(1, devices, finish, 0)


def local(noisy, strategy, county_hist, tract_county, tract_owner):
    units, regions = lax.axis_size("unit"), lax.axis_size("region")
    devices = units * regions
    rows, queries = noisy.shape
    width = strategy.shape[0]
    block = county_hist.shape[0]
    capacity = 2 * rows // devices
    pitch = -(-capacity // 8) * 8
    vmem = pl.BlockSpec(memory_space=pltpu.VMEM)
    released, relaid = pl.pallas_call(
        functools.partial(kernel, regions, units),
        out_shape=(
            jax.ShapeDtypeStruct((rows, queries), bf16),
            jax.ShapeDtypeStruct((devices, pitch, width), f32),
        ),
        in_specs=[pl.BlockSpec(memory_space=pltpu.HBM)] * 5,
        out_specs=(vmem, vmem),
        scratch_shapes=[
            pltpu.VMEM((rows, queries), bf16),
            pltpu.VMEM((block, width), f32),
            pltpu.VMEM((1, rows), i32),
            pltpu.VMEM((1, rows), i32),
            pltpu.VMEM((width, queries), bf16),
            pltpu.VMEM((queries, width), bf16),
            pltpu.VMEM((rows, width), f32),
            pltpu.VMEM((rows, width), bf16),
            pltpu.VMEM((rows, queries), bf16),
            pltpu.VMEM((units, block, queries + LANES), f32),
            pltpu.VMEM((units, block, queries + LANES), f32),
            pltpu.VMEM((units, block, width), f32),
            pltpu.VMEM((devices, pitch, width), f32),
            pltpu.VMEM((block, width), f32),
            pltpu.VMEM((block, queries), f32),
            pltpu.SemaphoreType.DMA((4,)),
            pltpu.SemaphoreType.DMA((width // TILE,)),
            pltpu.SemaphoreType.DMA((units,)),
            pltpu.SemaphoreType.DMA((units,)),
            pltpu.SemaphoreType.DMA((units,)),
            pltpu.SemaphoreType.DMA((units,)),
            pltpu.SemaphoreType.DMA((devices,)),
            pltpu.SemaphoreType.DMA((devices,)),
            pltpu.SemaphoreType.DMA,
        ],
        compiler_params=pltpu.CompilerParams(
            collective_id=0, has_side_effects=True, vmem_limit_bytes=46 * 2**20
        ),
    )(
        noisy,
        strategy,
        county_hist,
        tract_county.reshape(1, rows),
        tract_owner.reshape(1, rows),
    )
    return released, relaid[:, :capacity].reshape(devices * capacity, width)


def solution(mesh):
    both = ("region", "unit")
    in_specs = (P(both, None), P(), P(both, None), P(both), P(both, None))
    return jax.shard_map(
        local, mesh=mesh, in_specs=in_specs, out_specs=(P(both, None), P(both, None)), check_vma=False
    )
```

```python
import functools

import jax
import jax.numpy as jnp
from jax import lax
from jax.experimental import pallas as pl
from jax.experimental.pallas import tpu as pltpu
from jax.sharding import PartitionSpec as P

STEP = 0.25
TILE = 256
LANES = 128
MESH = pl.DeviceIdType.MESH
f32, bf16, i32 = jnp.float32, jnp.bfloat16, jnp.int32


def dot_nn(a, b):
    return lax.dot_general(a, b, (((1,), (0,)), ((), ())), preferred_element_type=f32)


def dot_nt(a, b):
    return lax.dot_general(a, b, (((1,), (1,)), ((), ())), preferred_element_type=f32)


def halves(x):
    high = x.astype(bf16)
    return high, (x - high.astype(f32)).astype(bf16)


def kernel(
    regions,
    units,
    noisy_in,
    strategy,
    hist_in,
    county_in,
    owner_in,
    released,
    relaid,
    noisy,
    hist,
    county_row,
    owner_row,
    matrix,
    turned,
    field,
    rounded,
    misfit,
    partial,
    gathered,
    gaps,
    slots,
    mean_step,
    mean_misfit,
    input_sem,
    load_sem,
    sum_send,
    sum_recv,
    gap_send,
    gap_recv,
    row_send,
    row_recv,
    own_sem,
):
    devices = regions * units
    region, unit = lax.axis_index("region"), lax.axis_index("unit")
    me = region * units + unit
    rows, queries = noisy.shape
    width = strategy.shape[0]
    block = hist.shape[0]
    counties = units * block
    pitch = slots.shape[1]

    inputs = [
        pltpu.make_async_copy(source, target, input_sem.at[i])
        for i, (source, target) in enumerate(
            [(county_in, county_row), (noisy_in, noisy), (hist_in, hist), (owner_in, owner_row)]
        )
    ]
    for copy in inputs:
        copy.start()

    def load(i):
        part = pl.ds(pl.multiple_of(i * TILE, TILE), TILE)
        return pltpu.make_async_copy(strategy.at[part], matrix.at[part], load_sem.at[i])

    lax.fori_loop(0, width // TILE, lambda i, c: (load(i).start(), c)[1], 0)

    barrier = pltpu.get_barrier_semaphore()

    def greet(k, c):
        peer = lax.rem(me + k, devices)
        pl.semaphore_signal(
            barrier, inc=1, device_id=(peer // units, lax.rem(peer, units)), device_id_type=MESH
        )
        return c

    lax.fori_loop(1, devices, greet, 0)

    def columns(i):
        return pl.ds(pl.multiple_of(i * TILE, TILE), TILE)

    for copy in inputs:
        copy.wait()
    local_row = county_row[...] - region * counties
    member_row = (
        lax.broadcasted_iota(i32, (counties, rows), 0) == jnp.broadcast_to(local_row, (counties, rows))
    )
    member_sum = member_row.astype(f32).astype(bf16)


    def sums(i, c):
        partial[:, :, columns(i)] = dot_nn(member_sum, noisy[:, columns(i)]).reshape(
            units, block, TILE
        )
        return c

    lax.fori_loop(0, queries // TILE, sums, 0)
    tally = jnp.sum(member_row.astype(f32), axis=1, keepdims=True)
    partial[:, :, queries:] = jnp.broadcast_to(tally, (counties, LANES)).reshape(units, block, LANES)

    pl.semaphore_wait(barrier, devices - 1)

    def to_unit(k):
        return lax.rem(unit + k, units), lax.rem(unit + units - k, units)

    def sum_copy(k):
        peer, _ = to_unit(k)
        return pltpu.make_async_remote_copy(
            src_ref=partial.at[peer],
            dst_ref=gathered.at[k],
            send_sem=sum_send.at[k],
            recv_sem=sum_recv.at[k],
            device_id=(region, peer),
            device_id_type=MESH,
        )

    for k in range(1, units):
        sum_copy(k).start()

    def first(i, c):
        load(i).wait()
        flipped = matrix[columns(i), :].T
        turned[:, columns(i)] = flipped
        value = STEP * dot_nn(noisy[...], flipped)
        field[:, columns(i)] = value
        rounded[:, columns(i)] = value.astype(bf16)
        return c

    lax.fori_loop(0, width // TILE, first, 0)

    def second(i, c):
        misfit[:, columns(i)] = dot_nn(rounded[...], matrix[:, columns(i)]).astype(bf16)
        return c

    lax.fori_loop(0, queries // TILE, second, 0)

    def third(i, c):
        field[:, columns(i)] = 2.0 * field[:, columns(i)] - STEP * dot_nn(
            misfit[...], turned[:, columns(i)]
        )
        return c

    lax.fori_loop(0, width // TILE, third, 0)
    owners = owner_row[...]
    hits = lax.broadcasted_iota(i32, (devices, rows), 0) == jnp.broadcast_to(owners, (devices, rows))
    before = lax.broadcasted_iota(i32, (rows, rows), 0) < lax.broadcasted_iota(i32, (rows, rows), 1)
    earlier = dot_nn(hits.astype(f32).astype(bf16), before.astype(f32).astype(bf16))
    slot = jnp.sum(earlier * hits.astype(f32), axis=0, keepdims=True).astype(i32)
    target = owners * pitch + slot
    place = (
        lax.broadcasted_iota(i32, (devices * pitch, rows), 0)
        == jnp.broadcast_to(target, (devices * pitch, rows))
    ).astype(f32).astype(bf16)
    diagonal = (
        lax.broadcasted_iota(i32, (rows, rows), 0) == lax.broadcasted_iota(i32, (rows, rows), 1)
    ).astype(f32).astype(bf16)
    member_col = dot_nt(diagonal, member_sum).astype(bf16)
    place_twice = jnp.concatenate([place, place], axis=1)
    county_place = dot_nt(place, member_sum).astype(bf16)
    county_twice = jnp.concatenate([county_place, county_place], axis=1)
    member_twice = jnp.concatenate([member_col, member_col], axis=1)

    for k in range(1, units):
        sum_copy(k).wait()
    total = partial[unit]
    for k in range(1, units):
        total = total + gathered[k]
    count = total[:, queries : queries + 1]
    mean = (total[:, :queries] / count).astype(bf16)

    def wide(i):
        return pl.ds(pl.multiple_of(i * 2 * TILE, 2 * TILE), 2 * TILE)

    def mean_first(i, c):
        mean_step[:, wide(i)] = STEP * dot_nn(mean, turned[:, wide(i)])
        return c

    lax.fori_loop(0, width // (2 * TILE), mean_first, 0)

    def mean_second(i, c):
        mean_misfit[:, wide(i)] = dot_nn(mean_step[...].astype(bf16), matrix[:, wide(i)])
        return c

    lax.fori_loop(0, queries // (2 * TILE), mean_second, 0)

    def mean_third(i, c):
        moved = 2.0 * mean_step[:, wide(i)] - STEP * dot_nn(
            mean_misfit[...].astype(bf16), turned[:, wide(i)]
        )
        gaps[unit, :, wide(i)] = hist[:, wide(i)] / count - moved
        return c

    lax.fori_loop(0, width // (2 * TILE), mean_third, 0)

    half = units // 2
    base = unit // half * half
    mirror = lax.rem(unit + half, units)

    def gap_copy(which, slot_at, peer):
        return pltpu.make_async_remote_copy(
            src_ref=gaps.at[slot_at],
            dst_ref=gaps.at[slot_at],
            send_sem=gap_send.at[which],
            recv_sem=gap_recv.at[which],
            device_id=(region, peer),
            device_id_type=MESH,
        )

    def ahead(k):
        return base + lax.rem(unit - base + k, half)

    gap_copy(0, unit, mirror).start()
    for k in range(1, half):
        gap_copy(k, unit, ahead(k)).start()

    def spread(i, c):
        pair = jnp.concatenate(halves(field[:, columns(i)]), axis=0)
        slots[:, :, columns(i)] = dot_nn(place_twice, pair).reshape(devices, pitch, TILE)
        return c

    lax.fori_loop(0, width // TILE, spread, 0)

    gap_copy(0, mirror, mirror).wait_recv()
    for k in range(1, half):
        gap_copy(half + k, mirror, ahead(k)).start()
    gap_copy(0, unit, mirror).wait_send()
    for k in range(1, half):
        source = ahead(half - k)
        gap_copy(k, unit, ahead(k)).wait_send()
        gap_copy(k, source, source).wait_recv()
        gap_copy(half + k, mirror, ahead(k)).wait_send()
        gap_copy(half + k, lax.rem(source + half, units), source).wait_recv()

    def last(i, c):
        pair = jnp.concatenate(halves(gaps[:, :, columns(i)].reshape(counties, TILE)), axis=0)
        slots[:, :, columns(i)] += dot_nn(county_twice, pair).reshape(devices, pitch, TILE)
        return c

    lax.fori_loop(0, width // TILE, last, 0)

    def row_copy(k):
        peer = lax.rem(me + k, devices)
        return pltpu.make_async_remote_copy(
            src_ref=slots.at[peer],
            dst_ref=relaid.at[me],
            send_sem=row_send.at[k],
            recv_sem=row_recv.at[k],
            device_id=(peer // units, lax.rem(peer, units)),
            device_id_type=MESH,
        )

    lax.fori_loop(1, devices, lambda k, c: (row_copy(k).start(), c)[1], 0)
    own = pltpu.make_async_copy(slots.at[me], relaid.at[me], own_sem)
    own.start()

    def settle(i, c):
        pair = jnp.concatenate(halves(gaps[:, :, columns(i)].reshape(counties, TILE)), axis=0)
        rounded[:, columns(i)] = (field[:, columns(i)] + dot_nn(member_twice, pair)).astype(bf16)
        return c

    lax.fori_loop(0, width // TILE, settle, 0)

    def release(i, c):
        released[:, columns(i)] = dot_nn(rounded[...], matrix[:, columns(i)]).astype(bf16)
        return c

    lax.fori_loop(0, queries // TILE, release, 0)
    own.wait()

    def finish(k, c):
        row_copy(k).wait_send()
        source = lax.rem(me + devices - k, devices)
        pltpu.make_async_remote_copy(
            src_ref=slots.at[me],
            dst_ref=relaid.at[source],
            send_sem=row_send.at[k],
            recv_sem=row_recv.at[k],
            device_id=(source // units, lax.rem(source, units)),
            device_id_type=MESH,
        ).wait_recv()
        return c

    lax.fori_loop(1, devices, finish, 0)


def local(noisy, strategy, county_hist, tract_county, tract_owner):
    units, regions = lax.axis_size("unit"), lax.axis_size("region")
    devices = units * regions
    rows, queries = noisy.shape
    width = strategy.shape[0]
    block = county_hist.shape[0]
    capacity = 2 * rows // devices
    pitch = -(-capacity // 8) * 8
    vmem = pl.BlockSpec(memory_space=pltpu.VMEM)
    released, relaid = pl.pallas_call(
        functools.partial(kernel, regions, units),
        out_shape=(
            jax.ShapeDtypeStruct((rows, queries), bf16),
            jax.ShapeDtypeStruct((devices, pitch, width), f32),
        ),
        in_specs=[pl.BlockSpec(memory_space=pltpu.HBM)] * 5,
        out_specs=(vmem, vmem),
        scratch_shapes=[
            pltpu.VMEM((rows, queries), bf16),
            pltpu.VMEM((block, width), f32),
            pltpu.VMEM((1, rows), i32),
            pltpu.VMEM((1, rows), i32),
            pltpu.VMEM((width, queries), bf16),
            pltpu.VMEM((queries, width), bf16),
            pltpu.VMEM((rows, width), f32),
            pltpu.VMEM((rows, width), bf16),
            pltpu.VMEM((rows, queries), bf16),
            pltpu.VMEM((units, block, queries + LANES), f32),
            pltpu.VMEM((units, block, queries + LANES), f32),
            pltpu.VMEM((units, block, width), f32),
            pltpu.VMEM((devices, pitch, width), f32),
            pltpu.VMEM((block, width), f32),
            pltpu.VMEM((block, queries), f32),
            pltpu.SemaphoreType.DMA((4,)),
            pltpu.SemaphoreType.DMA((width // TILE,)),
            pltpu.SemaphoreType.DMA((units,)),
            pltpu.SemaphoreType.DMA((units,)),
            pltpu.SemaphoreType.DMA((units,)),
            pltpu.SemaphoreType.DMA((units,)),
            pltpu.SemaphoreType.DMA((devices,)),
            pltpu.SemaphoreType.DMA((devices,)),
            pltpu.SemaphoreType.DMA,
        ],
        compiler_params=pltpu.CompilerParams(
            collective_id=0, has_side_effects=True, vmem_limit_bytes=46 * 2**20
        ),
    )(
        noisy,
        strategy,
        county_hist,
        tract_county.reshape(1, rows),
        tract_owner.reshape(1, rows),
    )
    return released, relaid[:, :capacity].reshape(devices * capacity, width)


def solution(mesh):
    both = ("region", "unit")
    in_specs = (P(both, None), P(), P(both, None), P(both), P(both, None))
    return jax.shard_map(
        local, mesh=mesh, in_specs=in_specs, out_specs=(P(both, None), P(both, None)), check_vma=False
    )
```

```python
import functools

import jax
import jax.numpy as jnp
from jax import lax
from jax.experimental import pallas as pl
from jax.experimental.pallas import tpu as pltpu
from jax.sharding import PartitionSpec as P

STEP = 0.25
TILE = 256
LANES = 128
MESH = pl.DeviceIdType.MESH
f32, bf16, i32 = jnp.float32, jnp.bfloat16, jnp.int32


def dot_nn(a, b):
    return lax.dot_general(a, b, (((1,), (0,)), ((), ())), preferred_element_type=f32)


def dot_nt(a, b):
    return lax.dot_general(a, b, (((1,), (1,)), ((), ())), preferred_element_type=f32)


def halves(x):
    high = x.astype(bf16)
    return high, (x - high.astype(f32)).astype(bf16)


def kernel(
    regions,
    units,
    noisy_in,
    strategy,
    hist_in,
    county_in,
    owner_in,
    released,
    relaid,
    noisy,
    hist,
    county_row,
    owner_row,
    matrix,
    turned,
    field,
    rounded,
    misfit,
    partial,
    gathered,
    gaps,
    slots,
    mean_step,
    mean_misfit,
    input_sem,
    load_sem,
    sum_send,
    sum_recv,
    gap_send,
    gap_recv,
    row_send,
    row_recv,
    own_sem,
):
    devices = regions * units
    region, unit = lax.axis_index("region"), lax.axis_index("unit")
    me = region * units + unit
    rows, queries = noisy.shape
    width = strategy.shape[0]
    block = hist.shape[0]
    counties = units * block
    pitch = slots.shape[1]

    inputs = [
        pltpu.make_async_copy(source, target, input_sem.at[i])
        for i, (source, target) in enumerate(
            [(county_in, county_row), (noisy_in, noisy), (hist_in, hist), (owner_in, owner_row)]
        )
    ]
    for copy in inputs:
        copy.start()

    def load(i):
        part = pl.ds(pl.multiple_of(i * TILE, TILE), TILE)
        return pltpu.make_async_copy(strategy.at[part], matrix.at[part], load_sem.at[i])

    lax.fori_loop(0, width // TILE, lambda i, c: (load(i).start(), c)[1], 0)

    barrier = pltpu.get_barrier_semaphore()

    def greet(k, c):
        peer = lax.rem(me + k, devices)
        pl.semaphore_signal(
            barrier, inc=1, device_id=(peer // units, lax.rem(peer, units)), device_id_type=MESH
        )
        return c

    lax.fori_loop(1, devices, greet, 0)

    def columns(i):
        return pl.ds(pl.multiple_of(i * TILE, TILE), TILE)

    for copy in inputs:
        copy.wait()
    local_row = county_row[...] - region * counties
    member_row = (
        lax.broadcasted_iota(i32, (counties, rows), 0) == jnp.broadcast_to(local_row, (counties, rows))
    )
    member_sum = member_row.astype(f32).astype(bf16)


    def sums(i, c):
        partial[:, :, columns(i)] = dot_nn(member_sum, noisy[:, columns(i)]).reshape(
            units, block, TILE
        )
        return c

    lax.fori_loop(0, queries // TILE, sums, 0)
    tally = jnp.sum(member_row.astype(f32), axis=1, keepdims=True)
    partial[:, :, queries:] = jnp.broadcast_to(tally, (counties, LANES)).reshape(units, block, LANES)

    pl.semaphore_wait(barrier, devices - 1)

    half = units // 2
    base = unit // half * half
    mirror = lax.rem(unit + half, units)

    def ahead(k):
        return base + lax.rem(unit - base + k, half)

    def sum_copy(which, block_at, peer):
        return pltpu.make_async_remote_copy(
            src_ref=partial.at[block_at],
            dst_ref=gathered.at[which],
            send_sem=sum_send.at[which],
            recv_sem=sum_recv.at[which],
            device_id=(region, peer),
            device_id_type=MESH,
        )

    def far_copy(k):
        return sum_copy(half + k, lax.rem(ahead(k) + half, units), ahead(k))

    for k in range(1, half):
        far_copy(k).start()
    for k in range(1, half):
        sum_copy(k, ahead(k), ahead(k)).start()

    def first(i, c):
        load(i).wait()
        flipped = matrix[columns(i), :].T
        turned[:, columns(i)] = flipped
        value = STEP * dot_nn(noisy[...], flipped)
        field[:, columns(i)] = value
        rounded[:, columns(i)] = value.astype(bf16)
        return c

    lax.fori_loop(0, width // TILE, first, 0)

    def second(i, c):
        misfit[:, columns(i)] = dot_nn(rounded[...], matrix[:, columns(i)]).astype(bf16)
        return c

    lax.fori_loop(0, queries // TILE, second, 0)

    for k in range(1, half):
        far_copy(k).wait()
    beyond = partial[mirror]
    for k in range(1, half):
        beyond = beyond + gathered[half + k]
    partial[mirror] = beyond
    sum_copy(0, mirror, mirror).start()

    def third(i, c):
        field[:, columns(i)] = 2.0 * field[:, columns(i)] - STEP * dot_nn(
            misfit[...], turned[:, columns(i)]
        )
        return c

    lax.fori_loop(0, width // TILE, third, 0)
    owners = owner_row[...]
    hits = lax.broadcasted_iota(i32, (devices, rows), 0) == jnp.broadcast_to(owners, (devices, rows))
    before = lax.broadcasted_iota(i32, (rows, rows), 0) < lax.broadcasted_iota(i32, (rows, rows), 1)
    earlier = dot_nn(hits.astype(f32).astype(bf16), before.astype(f32).astype(bf16))
    slot = jnp.sum(earlier * hits.astype(f32), axis=0, keepdims=True).astype(i32)
    target = owners * pitch + slot
    place = (
        lax.broadcasted_iota(i32, (devices * pitch, rows), 0)
        == jnp.broadcast_to(target, (devices * pitch, rows))
    ).astype(f32).astype(bf16)
    diagonal = (
        lax.broadcasted_iota(i32, (rows, rows), 0) == lax.broadcasted_iota(i32, (rows, rows), 1)
    ).astype(f32).astype(bf16)
    member_col = dot_nt(diagonal, member_sum).astype(bf16)
    place_twice = jnp.concatenate([place, place], axis=1)
    county_place = dot_nt(place, member_sum).astype(bf16)
    county_twice = jnp.concatenate([county_place, county_place], axis=1)
    member_twice = jnp.concatenate([member_col, member_col], axis=1)

    sum_copy(0, mirror, mirror).wait()
    for k in range(1, half):
        sum_copy(k, ahead(k), ahead(k)).wait()
    total = partial[unit] + gathered[0]
    for k in range(1, half):
        total = total + gathered[k]
    count = total[:, queries : queries + 1]
    mean = (total[:, :queries] / count).astype(bf16)

    def wide(i):
        return pl.ds(pl.multiple_of(i * 2 * TILE, 2 * TILE), 2 * TILE)

    def mean_first(i, c):
        mean_step[:, wide(i)] = STEP * dot_nn(mean, turned[:, wide(i)])
        return c

    lax.fori_loop(0, width // (2 * TILE), mean_first, 0)

    def mean_second(i, c):
        mean_misfit[:, wide(i)] = dot_nn(mean_step[...].astype(bf16), matrix[:, wide(i)])
        return c

    lax.fori_loop(0, queries // (2 * TILE), mean_second, 0)

    def mean_third(i, c):
        moved = 2.0 * mean_step[:, wide(i)] - STEP * dot_nn(
            mean_misfit[...].astype(bf16), turned[:, wide(i)]
        )
        gaps[unit, :, wide(i)] = hist[:, wide(i)] / count - moved
        return c

    lax.fori_loop(0, width // (2 * TILE), mean_third, 0)

    def gap_copy(which, slot_at, peer):
        return pltpu.make_async_remote_copy(
            src_ref=gaps.at[slot_at],
            dst_ref=gaps.at[slot_at],
            send_sem=gap_send.at[which],
            recv_sem=gap_recv.at[which],
            device_id=(region, peer),
            device_id_type=MESH,
        )

    gap_copy(0, unit, mirror).start()
    for k in range(1, half):
        gap_copy(k, unit, ahead(k)).start()

    def spread(i, c):
        pair = jnp.concatenate(halves(field[:, columns(i)]), axis=0)
        slots[:, :, columns(i)] = dot_nn(place_twice, pair).reshape(devices, pitch, TILE)
        return c

    lax.fori_loop(0, width // TILE, spread, 0)

    gap_copy(0, mirror, mirror).wait_recv()
    for k in range(1, half):
        gap_copy(half + k, mirror, ahead(k)).start()
    gap_copy(0, unit, mirror).wait_send()
    for k in range(1, half):
        source = ahead(half - k)
        gap_copy(k, unit, ahead(k)).wait_send()
        gap_copy(k, source, source).wait_recv()
        gap_copy(half + k, mirror, ahead(k)).wait_send()
        gap_copy(half + k, lax.rem(source + half, units), source).wait_recv()

    def last(i, c):
        pair = jnp.concatenate(halves(gaps[:, :, columns(i)].reshape(counties, TILE)), axis=0)
        slots[:, :, columns(i)] += dot_nn(county_twice, pair).reshape(devices, pitch, TILE)
        return c

    lax.fori_loop(0, width // TILE, last, 0)

    def row_copy(k):
        peer = lax.rem(me + k, devices)
        return pltpu.make_async_remote_copy(
            src_ref=slots.at[peer],
            dst_ref=relaid.at[me],
            send_sem=row_send.at[k],
            recv_sem=row_recv.at[k],
            device_id=(peer // units, lax.rem(peer, units)),
            device_id_type=MESH,
        )

    lax.fori_loop(1, devices, lambda k, c: (row_copy(k).start(), c)[1], 0)
    own = pltpu.make_async_copy(slots.at[me], relaid.at[me], own_sem)
    own.start()

    def settle(i, c):
        pair = jnp.concatenate(halves(gaps[:, :, columns(i)].reshape(counties, TILE)), axis=0)
        rounded[:, columns(i)] = (field[:, columns(i)] + dot_nn(member_twice, pair)).astype(bf16)
        return c

    lax.fori_loop(0, width // TILE, settle, 0)

    def release(i, c):
        released[:, columns(i)] = dot_nn(rounded[...], matrix[:, columns(i)]).astype(bf16)
        return c

    lax.fori_loop(0, queries // TILE, release, 0)
    own.wait()

    def finish(k, c):
        row_copy(k).wait_send()
        source = lax.rem(me + devices - k, devices)
        pltpu.make_async_remote_copy(
            src_ref=slots.at[me],
            dst_ref=relaid.at[source],
            send_sem=row_send.at[k],
            recv_sem=row_recv.at[k],
            device_id=(source // units, lax.rem(source, units)),
            device_id_type=MESH,
        ).wait_recv()
        return c

    lax.fori_loop(1, devices, finish, 0)


def local(noisy, strategy, county_hist, tract_county, tract_owner):
    units, regions = lax.axis_size("unit"), lax.axis_size("region")
    devices = units * regions
    rows, queries = noisy.shape
    width = strategy.shape[0]
    block = county_hist.shape[0]
    capacity = 2 * rows // devices
    pitch = -(-capacity // 8) * 8
    vmem = pl.BlockSpec(memory_space=pltpu.VMEM)
    released, relaid = pl.pallas_call(
        functools.partial(kernel, regions, units),
        out_shape=(
            jax.ShapeDtypeStruct((rows, queries), bf16),
            jax.ShapeDtypeStruct((devices, pitch, width), f32),
        ),
        in_specs=[pl.BlockSpec(memory_space=pltpu.HBM)] * 5,
        out_specs=(vmem, vmem),
        scratch_shapes=[
            pltpu.VMEM((rows, queries), bf16),
            pltpu.VMEM((block, width), f32),
            pltpu.VMEM((1, rows), i32),
            pltpu.VMEM((1, rows), i32),
            pltpu.VMEM((width, queries), bf16),
            pltpu.VMEM((queries, width), bf16),
            pltpu.VMEM((rows, width), f32),
            pltpu.VMEM((rows, width), bf16),
            pltpu.VMEM((rows, queries), bf16),
            pltpu.VMEM((units, block, queries + LANES), f32),
            pltpu.VMEM((units, block, queries + LANES), f32),
            pltpu.VMEM((units, block, width), f32),
            pltpu.VMEM((devices, pitch, width), f32),
            pltpu.VMEM((block, width), f32),
            pltpu.VMEM((block, queries), f32),
            pltpu.SemaphoreType.DMA((4,)),
            pltpu.SemaphoreType.DMA((width // TILE,)),
            pltpu.SemaphoreType.DMA((units,)),
            pltpu.SemaphoreType.DMA((units,)),
            pltpu.SemaphoreType.DMA((units,)),
            pltpu.SemaphoreType.DMA((units,)),
            pltpu.SemaphoreType.DMA((devices,)),
            pltpu.SemaphoreType.DMA((devices,)),
            pltpu.SemaphoreType.DMA,
        ],
        compiler_params=pltpu.CompilerParams(
            collective_id=0, has_side_effects=True, vmem_limit_bytes=46 * 2**20
        ),
    )(
        noisy,
        strategy,
        county_hist,
        tract_county.reshape(1, rows),
        tract_owner.reshape(1, rows),
    )
    return released, relaid[:, :capacity].reshape(devices * capacity, width)


def solution(mesh):
    both = ("region", "unit")
    in_specs = (P(both, None), P(), P(both, None), P(both), P(both, None))
    return jax.shard_map(
        local, mesh=mesh, in_specs=in_specs, out_specs=(P(both, None), P(both, None)), check_vma=False
    )
```
